32 devices in a mesh: group: 2 (over y), seq: 4 (over z), shard: 2 (over x), guide: 2 (over core).
Axes of the slice: x: 2, y: 2, z: 4, core: 2. Of those that a mesh axis runs over, the one named last changes fastest.
Arguments:
- queries: bfloat16 [2, 2, 512, 2560], P('guide', 'group', 'seq', 'shard'), parts along dimension 1, may hold values from -120 to 120
- key_vecs: bfloat16 [2, 2, 512, 2560], P('guide', 'group', 'seq', 'shard'), parts along dimension 1, may hold values from -4 to 4
- value_vecs: bfloat16 [2, 2, 512, 2560], P('guide', 'group', 'seq', 'shard'), parts along dimension 1, may hold values from -24 to 24
- residual: bfloat16 [2, 2, 512, 5120], P('guide', 'group', 'seq', 'shard'), parts along dimension 1, may hold values from -64 to 64
- w_out: bfloat16 [2560, 5120], P('shard', 'guide'), may hold values from -0.125 to 0.125
- attn_gate: float32 [2, 5120], P('group', 'shard'), parts along dimension 0, may hold values from 2 to 4
- norm_shift: float32 [2, 5120], P('group', 'shard'), parts along dimension 0, may hold values from -3 to 3
- norm_scale: float32 [2, 5120], P('group', 'shard'), parts along dimension 0, may hold values from -2.5 to 2.5
- w_head: bfloat16 [5120, 64], P('shard'), may hold values from -0.078125 to 0.078125
- noise: float32 [2, 4, 128, 64], P('group', 'seq', None, 'guide'), parts along dimension 0, may hold values from -6 to 6
- timesteps: int32 [2], P('group'), parts along dimension 0, may hold values from 100 to 980
- frame_owner: int32 [2, 4], P('group'), parts along dimension 0, may hold values from 0 to 3, each once within a row
Outputs:
- sds_grad: float32 [2, 4, 128, 64], P('group', 'seq', None, 'guide'), parts along dimension 0
The draws below stay inside these ranges and needn't reach their ends.
There are 2 independent parts, one for each index of `group`. The reference program is written for one: setup_inputs(seed, part) draws one part's arguments, and reference() takes and returns one part's arrays. A program takes and returns all parts, laid end to end along the dimension named above; an argument that names none is the same for every part. Nothing has to cross between parts.
Inputs may be any that keep to these rules, and one draw needn't show every extreme that they name: `frame_owner`: each row names every owner index once.
All inputs are finite; a program needn't handle non-finite values.
Results may differ from the reference program's by a relative error of at most 0.003.
Values may be sent and summed in bfloat16 or wider, within the bound.
A program may use at most 128 MiB of HBM per device.

```python
import jax
import jax.numpy as jnp
from jax import lax

D = 5120
HEAD_DIM = 128
HEADS = 20
OUT_CH = 64
TSTEPS = 1
SEG = 512
FRAMES = 4
FR_GRP = 32
FTOK = 128
N_SEQ = 4


def attention_pair(base):
    shape = (2, TSTEPS, SEG, HEADS * HEAD_DIM)
    keys_raw = jnp.clip(jax.random.normal(jax.random.fold_in(base, 103), shape, jnp.float32), -4.0, 4.0)
    query_raw = 1.5 * jnp.clip(jax.random.normal(jax.random.fold_in(base, 104), shape, jnp.float32), -4.0, 4.0)
    return (query_raw, keys_raw)


def draw_queries(key, part):
    return attention_pair(key)[0].astype(jnp.bfloat16)


def draw_key_vecs(key, part):
    return attention_pair(key)[1].astype(jnp.bfloat16)


def draw_residual(key, part):
    shape = (2, TSTEPS, SEG, D)
    position = jnp.arange(D, dtype=jnp.int32).astype(jnp.float32) / D
    spread = 0.4 * jnp.exp(jax.random.uniform(jax.random.fold_in(key, 201), (D,), jnp.float32, 0.0, 2.302585))
    rising = jnp.exp(position * 1.098612)
    entries = jnp.clip(jax.random.normal(jax.random.fold_in(key, 203), shape, jnp.float32), -4.0, 4.0)
    return (entries * spread * rising).astype(jnp.bfloat16)


def steps_of(stream_key, dims, split, least, top_value):
    def one(axis_at, blocks):
        draws = jax.random.uniform(jax.random.fold_in(jax.random.fold_in(stream_key, 6), axis_at), (blocks,), jnp.float32, least / len(split), top_value / len(split))
        return jnp.repeat(jnp.exp(draws), dims[axis_at] // blocks).reshape((-1,) + (1,) * (len(dims) - axis_at - 1))

    level = one(*split[0])
    for cut in split[1:]:
        level = level * one(*cut)
    return level


def scatter_about(rng, shape, deviation, most, cuts=(), kind=jnp.bfloat16):
    gain = steps_of(rng, shape, cuts, -0.22, 0.18) if cuts else 1.0
    values = jax.random.normal(rng, shape, jnp.float32) * deviation * gain
    return jnp.minimum(jnp.maximum(values, -most), most).astype(kind)


def setup_inputs(seed: int = 0, part: int = 0) -> dict:
    arg_keys = jax.random.split(jax.random.key(seed), 13)
    own_keys = jax.random.split(jax.random.fold_in(arg_keys[12], part), 13)
    return {
        "queries": draw_queries(jax.random.fold_in(jax.random.fold_in(arg_keys[12], part), 71), part),
        "key_vecs": draw_key_vecs(jax.random.fold_in(jax.random.fold_in(arg_keys[12], part), 71), part),
        "value_vecs": scatter_about(own_keys[2], (2, TSTEPS, SEG, HEADS * HEAD_DIM), 4.0, 24.0, ((0, 2), (2, 4), (3, 2))),
        "residual": draw_residual(jax.random.fold_in(jax.random.fold_in(arg_keys[12], part), 71), part),
        "w_out": scatter_about(arg_keys[4], (HEADS * HEAD_DIM, D), (HEADS * HEAD_DIM) ** -0.5, 0.125, ((0, 2), (1, 2))),
        "attn_gate": jnp.clip(2.0 + 2.0 * jax.random.uniform(own_keys[5], (TSTEPS, D), jnp.float32) ** steps_of(own_keys[5], (TSTEPS, D), ((1, 2),), -0.2, 0.2), 2.0, 4.0),
        "norm_shift": scatter_about(own_keys[6], (TSTEPS, D), 0.5, 3.0, ((1, 2),), jnp.float32),
        "norm_scale": scatter_about(own_keys[7], (TSTEPS, D), 0.5, 2.5, ((1, 2),), jnp.float32),
        "w_head": scatter_about(arg_keys[8], (D, OUT_CH), D ** -0.5, 0.078125, ((0, 2),)),
        "noise": scatter_about(own_keys[9], (TSTEPS, FRAMES, FTOK, OUT_CH), 1.0, 6.0, ((1, 4), (3, 2)), jnp.float32),
        "timesteps": jax.random.randint(own_keys[10], (TSTEPS,), 100, 981).astype(jnp.int32),
        "frame_owner": jax.vmap(lambda own: jax.random.permutation(own, FRAMES))(jax.random.split(own_keys[11], TSTEPS)).reshape((TSTEPS, FRAMES)).astype(jnp.int32),
    }


beta_low = 0.0001
beta_high = 0.02
guidance_scale = 3.0
norm_epsilon = 1e-06

def plan_weight(timesteps):
    steps_float = timesteps.astype(jnp.float32)
    exponent = (steps_float + 1.0) * beta_low + (beta_high - beta_low) * steps_float * (steps_float + 1.0) / (2.0 * 999.0)
    return 1.0 - jnp.exp(-exponent)

def attend_head(operands):
    query_one, key_one, value_one = operands
    query_float = query_one.astype(jnp.float32)
    key_float = key_one.astype(jnp.float32)
    value_float = value_one.astype(jnp.float32)
    scores = jnp.einsum('qd,kd->qk', query_float, key_float) * HEAD_DIM ** (-0.5)
    highest = lax.optimization_barrier(jnp.max(scores, axis=-1, keepdims=True))
    expo = jnp.exp(scores - highest)
    denominator = lax.optimization_barrier(jnp.sum(expo, axis=-1))
    rounded = expo.astype(jnp.bfloat16).astype(jnp.float32)
    mixed = jnp.einsum('qk,kd->qd', rounded, value_float) / denominator[:, None]
    return mixed.astype(jnp.bfloat16)

def split_heads(array):
    return array.reshape(2 * TSTEPS, SEG, HEADS, HEAD_DIM).transpose(0, 2, 1, 3).reshape(2 * TSTEPS * HEADS, SEG, HEAD_DIM)

def reference(queries, key_vecs, value_vecs, residual, w_out, attn_gate, norm_shift, norm_scale, w_head, noise, timesteps, frame_owner):
    width_heads = HEADS * HEAD_DIM
    stacked = (split_heads(queries), split_heads(key_vecs), split_heads(value_vecs))
    per_head = lax.map(attend_head, stacked)
    attended = per_head.reshape(2 * TSTEPS, HEADS, SEG, HEAD_DIM).transpose(0, 2, 1, 3).reshape(2 * TSTEPS * SEG, width_heads)
    projected = jnp.dot(attended, w_out, preferred_element_type=jnp.float32)
    hidden = residual.astype(jnp.float32) + attn_gate[None, :, None, :] * projected.reshape(2, TSTEPS, SEG, D)
    mean_row = lax.optimization_barrier(jnp.mean(hidden, axis=-1, keepdims=True))
    var_row = lax.optimization_barrier(jnp.mean(hidden * hidden, axis=-1, keepdims=True)) - mean_row * mean_row
    modulated = (hidden - mean_row) * lax.rsqrt(var_row + norm_epsilon) * (1.0 + norm_scale[None, :, None, :]) + norm_shift[None, :, None, :]
    predicted = jnp.dot(modulated.reshape(2 * TSTEPS * SEG, D), w_head.astype(jnp.float32), precision=lax.Precision.HIGHEST).reshape(2, TSTEPS, SEG, OUT_CH)
    guided = predicted[1] + guidance_scale * (predicted[0] - predicted[1])
    framed = guided.reshape(TSTEPS, N_SEQ, N_SEQ, FR_GRP, OUT_CH).transpose(0, 2, 1, 3, 4).reshape(TSTEPS, FRAMES, FTOK, OUT_CH)
    owner_table = (frame_owner[:, :, None] == jnp.arange(FRAMES, dtype=jnp.int32)[None, None, :]).astype(jnp.float32)
    by_owner = jnp.einsum('tfo,tfgc->togc', owner_table, framed, precision=lax.Precision.HIGHEST)
    weight = plan_weight(timesteps)
    return weight[:, None, None, None] * (by_owner - noise)
```

```python
import functools
import math

import jax
import jax.numpy as jnp
from jax import lax
from jax.experimental import pallas as pl
from jax.experimental.pallas import tpu as pltpu
from jax.sharding import PartitionSpec as P

HEAD_DIM = 128
MESH = pl.DeviceIdType.MESH

beta_low = 0.0001
beta_high = 0.02
guidance_scale = 3.0
norm_epsilon = 1e-06


def plan_weight(timesteps):
    steps_float = timesteps.astype(jnp.float32)
    exponent = (steps_float + 1.0) * beta_low + (beta_high - beta_low) * steps_float * (
        steps_float + 1.0
    ) / (2.0 * 999.0)
    return 1.0 - jnp.exp(-exponent)


def attend(q, k, v):
    scores = lax.dot_general(q, k, (((1,), (1,)), ((), ())), preferred_element_type=jnp.float32)
    top = jnp.max(scores, axis=-1, keepdims=True)
    expo = jnp.exp2((scores - top) * (HEAD_DIM ** (-0.5) * math.log2(math.e)))
    denom = jnp.sum(expo, axis=-1, keepdims=True)
    mixed = jnp.dot(expo.astype(jnp.bfloat16), v, preferred_element_type=jnp.float32)
    return (mixed / denom).astype(jnp.bfloat16)


def kernel(
    n_seq, n_shard, width_all, chunk,
    q_hbm, k_hbm, v_hbm, res_hbm, w_hbm, gate_hbm, shift_hbm, scale_hbm, wh_hbm, noise_hbm,
    steps_ref, owner_ref, out_ref,
    qkv, left, q_left, att, ostage, w_vm, res_vm, vec_vm, wh_vm, noise_vm,
    psend, pbuf, msg, gbuf, fsend,
    z_send, z_recv, l_send, l_recv, o_send, o_recv, a_send, a_recv,
    p_send, p_recv, m_send, m_recv, f_send, f_recv, in_sem, own_sem,
):
    z, s, g = lax.axis_index("seq"), lax.axis_index("shard"), lax.axis_index("guide")
    rows, width = q_hbm.shape
    heads = width // HEAD_DIM
    n_full = heads // n_seq
    n_left = heads - n_full * n_seq
    left_at = n_full * n_seq * HEAD_DIM
    half = w_hbm.shape[1]
    feats = res_hbm.shape[1]
    per = half // feats
    n_chunk = feats // chunk
    channels = wh_hbm.shape[1]
    n_frame = owner_ref.shape[1]
    frame_rows = rows // n_frame

    def head_cols(index):
        return pl.ds(pl.multiple_of(index * HEAD_DIM, HEAD_DIM), HEAD_DIM)

    def block_rows(index):
        return pl.ds(pl.multiple_of(index * rows, rows), rows)

    def ahead(d):
        return lax.rem(z + d, n_seq)

    def behind(d):
        return lax.rem(z + n_seq - d, n_seq)

    own = []
    tensors = (q_hbm, k_hbm, v_hbm)
    for a in range(n_full):
        for t in range(3):
            own.append(pltpu.make_async_copy(
                tensors[t].at[:, head_cols(z * n_full + a)], qkv.at[a, t, block_rows(z)],
                own_sem.at[a * 3 + t]))
    if n_left:
        for t in range(2):
            own.append(pltpu.make_async_copy(
                tensors[t + 1].at[:, pl.ds(left_at, n_left * HEAD_DIM)], left.at[t, block_rows(z)],
                own_sem.at[n_full * 3 + t]))
        own.append(pltpu.make_async_copy(
            q_hbm.at[:, pl.ds(left_at, n_left * HEAD_DIM)], q_left, own_sem.at[n_full * 3 + 2]))
    loads = [
        pltpu.make_async_copy(gate_hbm, vec_vm.at[0], in_sem.at[0]),
        pltpu.make_async_copy(shift_hbm, vec_vm.at[1], in_sem.at[1]),
        pltpu.make_async_copy(scale_hbm, vec_vm.at[2], in_sem.at[2]),
        pltpu.make_async_copy(wh_hbm, wh_vm, in_sem.at[3]),
        pltpu.make_async_copy(noise_hbm, noise_vm, in_sem.at[4]),
        pltpu.make_async_copy(res_hbm, res_vm, in_sem.at[5]),
        pltpu.make_async_copy(w_hbm, w_vm, in_sem.at[6]),
    ]

    barrier = pltpu.get_barrier_semaphore()
    for d in range(1, n_seq):
        pl.semaphore_signal(barrier, inc=1, device_id={"seq": ahead(d)}, device_id_type=MESH)
    n_local = 2 * n_shard
    me_local = s * 2 + g

    def local_peer(d):
        index = lax.rem(me_local + d, n_local)
        return {"shard": index // 2, "guide": index % 2}

    for d in range(1, n_local):
        pl.semaphore_signal(barrier, inc=1, device_id=local_peer(d), device_id_type=MESH)
    for copy in own:
        copy.start()
    pl.semaphore_wait(barrier, n_seq - 1 + n_local - 1)

    order = sorted(range(1, n_seq), key=lambda d: -min(d, n_seq - d))
    z_copies = {}
    for a in range(n_full):
        for d in order:
            for t in range(3):
                copy = pltpu.make_async_remote_copy(
                    src_ref=tensors[t].at[:, head_cols(ahead(d) * n_full + a)],
                    dst_ref=qkv.at[a, t, block_rows(z)],
                    send_sem=z_send.at[a, t, d - 1], recv_sem=z_recv.at[a, t, d - 1],
                    device_id={"seq": ahead(d)}, device_id_type=MESH)
                copy.start()
                z_copies[a, d, t] = copy
    l_copies = []
    if n_left:
        for d in order:
            for t in range(2):
                copy = pltpu.make_async_remote_copy(
                    src_ref=tensors[t + 1].at[:, pl.ds(left_at, n_left * HEAD_DIM)],
                    dst_ref=left.at[t, block_rows(z)],
                    send_sem=l_send.at[t, d - 1], recv_sem=l_recv.at[t, d - 1],
                    device_id={"seq": ahead(d)}, device_id_type=MESH)
                copy.start()
                l_copies.append(copy)
    for copy in loads:
        copy.start()

    for copy in loads[:6]:
        copy.wait()
    gains = jnp.concatenate([1.0 + vec_vm[2], vec_vm[1]], axis=0)
    consts = jnp.dot(
        gains, wh_vm[...].astype(jnp.float32),
        precision=lax.Precision.HIGHEST, preferred_element_type=jnp.float32)
    msg[me_local, rows:, :] = jnp.zeros((8, msg.shape[2]), jnp.float32)
    msg[me_local, rows : rows + 2, 0:channels] = consts
    for copy in own:
        copy.wait()

    o_copies = []
    for a in range(n_full):
        for d in range(1, n_seq):
            for t in range(3):
                z_copies[a, d, t].wait_recv()
        for d in order + [0]:
            to = ahead(d)
            mixed = attend(qkv[a, 0, block_rows(to)], qkv[a, 1], qkv[a, 2])
            cols = head_cols(z * n_full + a)
            if d == 0:
                att[g, :, cols] = mixed
            else:
                ostage[a, d - 1] = mixed
                copy = pltpu.make_async_remote_copy(
                    src_ref=ostage.at[a, d - 1], dst_ref=att.at[g, :, cols],
                    send_sem=o_send.at[a, d - 1], recv_sem=o_recv.at[a, d - 1],
                    device_id={"seq": to}, device_id_type=MESH)
                copy.start()
                o_copies.append(copy)
    for copy in l_copies:
        copy.wait_recv()
    for h in range(n_left):
        cols = pl.ds(h * HEAD_DIM, HEAD_DIM)
        att[g, :, pl.ds(left_at + h * HEAD_DIM, HEAD_DIM)] = attend(
            q_left[:, cols], left[0, :, cols], left[1, :, cols])
    for a in range(n_full):
        for d in range(1, n_seq):
            pltpu.make_async_remote_copy(
                src_ref=ostage.at[a, d - 1], dst_ref=att.at[g, :, head_cols(behind(d) * n_full + a)],
                send_sem=o_send.at[a, d - 1], recv_sem=o_recv.at[a, d - 1],
                device_id={"seq": ahead(d)}, device_id_type=MESH).wait_recv()

    swap = pltpu.make_async_remote_copy(
        src_ref=att.at[g], dst_ref=att.at[g], send_sem=a_send, recv_sem=a_recv,
        device_id={"guide": 1 - g}, device_id_type=MESH)
    swap.start()
    loads[6].wait()
    swap.wait_recv()

    def p_copy(b, q, c):
        return pltpu.make_async_remote_copy(
            src_ref=psend.at[b, q, c], dst_ref=pbuf.at[s, c],
            send_sem=p_send.at[b, q, c], recv_sem=p_recv.at[s, c],
            device_id={"shard": g * per + q, "guide": b}, device_id_type=MESH)

    def is_me(b, q):
        return jnp.logical_and(g == b, g * per + q == s)

    both = jnp.concatenate([att[0], att[1]], axis=0)
    for c in range(n_chunk):
        for q in range(per):
            part = jnp.dot(
                both, w_vm[:, q * feats + c * chunk : q * feats + (c + 1) * chunk],
                preferred_element_type=jnp.float32).astype(jnp.bfloat16)
            for b in range(2):
                psend[b, q, c] = part[b * rows : (b + 1) * rows]

                @pl.when(is_me(b, q))
                def _():
                    pbuf[s, c] = psend[b, q, c]

                @pl.when(jnp.logical_not(is_me(b, q)))
                def _():
                    p_copy(b, q, c).start()

    from_guide = s // per
    first = jnp.zeros((rows, 1), jnp.float32)
    second = jnp.zeros((rows, 1), jnp.float32)
    head = jnp.zeros((rows, channels), jnp.float32)
    for c in range(n_chunk):
        for r in range(n_shard):

            @pl.when(jnp.logical_not(jnp.logical_and(from_guide == g, s == r)))
            def _():
                pltpu.make_async_remote_copy(
                    src_ref=psend.at[0, 0, c], dst_ref=pbuf.at[r, c],
                    send_sem=p_send.at[0, 0, c], recv_sem=p_recv.at[r, c],
                    device_id={"guide": 1 - g}, device_id_type=MESH).wait_recv()

        at = slice(c * chunk, (c + 1) * chunk)
        total = pbuf[0, c].astype(jnp.float32)
        for r in range(1, n_shard):
            total = total + pbuf[r, c].astype(jnp.float32)
        hidden = res_vm[:, at].astype(jnp.float32) + vec_vm[0, :, at] * total
        first = first + jnp.sum(hidden, axis=-1, keepdims=True)
        second = second + jnp.sum(hidden * hidden, axis=-1, keepdims=True)
        gained = hidden * (1.0 + vec_vm[2, :, at])
        high = gained.astype(jnp.bfloat16)
        rest = gained - high.astype(jnp.float32)
        low = rest.astype(jnp.bfloat16)
        last = (rest - low.astype(jnp.float32)).astype(jnp.bfloat16)
        wh = wh_vm[c * chunk : (c + 1) * chunk, :]
        for piece in (last, low, high):
            head = head + jnp.dot(piece, wh, preferred_element_type=jnp.float32)
    msg[me_local, 0:rows, 0:channels] = head
    tail = msg.shape[2] - channels
    lane = lax.broadcasted_iota(jnp.int32, (rows, tail), 1)
    msg[me_local, 0:rows, channels:] = jnp.where(lane == 0, first, second)
    m_copies = []
    for d in range(1, n_local):
        copy = pltpu.make_async_remote_copy(
            src_ref=msg.at[me_local], dst_ref=msg.at[me_local],
            send_sem=m_send.at[d - 1], recv_sem=m_recv.at[d - 1],
            device_id=local_peer(d), device_id_type=MESH)
        copy.start()
        m_copies.append(copy)
    for copy in m_copies:
        copy.wait_recv()

    eps = []
    for b in range(2):
        total = msg[b]
        for r in range(1, n_shard):
            total = total + msg[r * 2 + b]
        mean = total[0:rows, channels : channels + 1] / width_all
        var = total[0:rows, channels + 1 : channels + 2] / width_all - mean * mean
        inv = lax.rsqrt(var + norm_epsilon)
        eps.append(
            (total[0:rows, 0:channels] - mean * total[rows : rows + 1, 0:channels]) * inv
            + total[rows + 1 : rows + 2, 0:channels])
    guided = eps[1] + guidance_scale * (eps[0] - eps[1])

    f_copies = []
    for d in order + [0]:
        to = ahead(d)
        picked = jnp.zeros((frame_rows, channels), jnp.float32)
        for f in range(n_frame):
            hit = jnp.full((1, channels), owner_ref[0, f], jnp.int32) == to
            picked = picked + jnp.where(hit, guided[f * frame_rows : (f + 1) * frame_rows], 0.0)
        if d == 0:
            gbuf[z] = picked
        else:
            fsend[d - 1] = picked
            copy = pltpu.make_async_remote_copy(
                src_ref=fsend.at[d - 1], dst_ref=gbuf.at[z],
                send_sem=f_send.at[d - 1], recv_sem=f_recv.at[d - 1],
                device_id={"seq": to}, device_id_type=MESH)
            copy.start()
            f_copies.append(copy)
    out_ch = channels // 2
    weight = plan_weight(jnp.full((1, out_ch), steps_ref[0], jnp.int32))
    for copy in f_copies:
        copy.wait_recv()
    is_first = jnp.full((1, out_ch), g, jnp.int32) == 0
    for r in range(n_seq):
        rows_r = slice(r * frame_rows, (r + 1) * frame_rows)
        mine = jnp.where(is_first, gbuf[r, :, 0:out_ch], gbuf[r, :, out_ch:])
        out_ref[rows_r, :] = weight * (mine - noise_vm[rows_r, :])

    for copy in list(z_copies.values()) + l_copies + o_copies + m_copies + f_copies + [swap]:
        copy.wait_send()
    for c in range(n_chunk):
        for q in range(per):
            for b in range(2):

                @pl.when(jnp.logical_not(is_me(b, q)))
                def _():
                    p_copy(b, q, c).wait_send()


def on_device(
    n_seq, n_shard,
    queries, key_vecs, value_vecs, residual, w_out, attn_gate, norm_shift, norm_scale, w_head,
    noise, timesteps, frame_owner,
):
    rows, width = queries.shape[2:]
    heads = width // HEAD_DIM
    n_full = heads // n_seq
    n_left = heads - n_full * n_seq
    half = w_out.shape[1]
    feats = residual.shape[3]
    per = half // feats
    chunk = next(size for size in (512, 256, 128) if feats % size == 0)
    n_chunk = feats // chunk
    channels = w_head.shape[1]
    n_frame = frame_owner.shape[1]
    frame_rows = rows // n_frame
    n_local = 2 * n_shard
    bf16, f32 = jnp.bfloat16, jnp.float32
    full1, left1 = max(n_full, 1), max(n_left, 1)
    dma = pltpu.SemaphoreType.DMA
    hbm = pl.BlockSpec(memory_space=pl.ANY)
    smem = pl.BlockSpec(memory_space=pltpu.SMEM)
    out = pl.pallas_call(
        functools.partial(kernel, n_seq, n_shard, feats * n_shard, chunk),
        out_shape=jax.ShapeDtypeStruct(noise.shape[2:], f32),
        in_specs=[hbm] * 10 + [smem, smem],
        out_specs=pl.BlockSpec(memory_space=pltpu.VMEM),
        scratch_shapes=[
            pltpu.VMEM((full1, 3, n_seq * rows, HEAD_DIM), bf16),
            pltpu.VMEM((2, n_seq * rows, left1 * HEAD_DIM), bf16),
            pltpu.VMEM((rows, left1 * HEAD_DIM), bf16),
            pltpu.VMEM((2, rows, width), bf16),
            pltpu.VMEM((full1, n_seq - 1, rows, HEAD_DIM), bf16),
            pltpu.VMEM(w_out.shape, bf16),
            pltpu.VMEM((rows, feats), bf16),
            pltpu.VMEM((3, 1, feats), f32),
            pltpu.VMEM(w_head.shape, bf16),
            pltpu.VMEM(noise.shape[2:], f32),
            pltpu.VMEM((2, per, n_chunk, rows, chunk), bf16),
            pltpu.VMEM((n_shard, n_chunk, rows, chunk), bf16),
            pltpu.VMEM((n_local, rows + 8, 128), f32),
            pltpu.VMEM((n_seq, frame_rows, channels), f32),
            pltpu.VMEM((n_seq - 1, frame_rows, channels), f32),
            dma((full1, 3, n_seq - 1)), dma((full1, 3, n_seq - 1)),
            dma((2, n_seq - 1)), dma((2, n_seq - 1)),
            dma((full1, n_seq - 1)), dma((full1, n_seq - 1)),
            dma, dma,
            dma((2, per, n_chunk)), dma((n_shard, n_chunk)),
            dma((n_local - 1,)), dma((n_local - 1,)),
            dma((n_seq - 1,)), dma((n_seq - 1,)),
            dma((7,)), dma((n_full * 3 + 3,)),
        ],
        compiler_params=pltpu.CompilerParams(
            collective_id=0, has_side_effects=True, vmem_limit_bytes=48 * 1024 * 1024),
    )(
        queries[0, 0], key_vecs[0, 0], value_vecs[0, 0], residual[0, 0], w_out,
        attn_gate, norm_shift, norm_scale, w_head, noise[0, 0], timesteps, frame_owner,
    )
    return out[None, None]


def solution(mesh):
    return jax.shard_map(
        functools.partial(on_device, mesh.shape["seq"], mesh.shape["shard"]),
        mesh=mesh,
        in_specs=(
            P("guide", "group", "seq", "shard"),
            P("guide", "group", "seq", "shard"),
            P("guide", "group", "seq", "shard"),
            P("guide", "group", "seq", "shard"),
            P("shard", "guide"),
            P("group", "shard"),
            P("group", "shard"),
            P("group", "shard"),
            P("shard", None),
            P("group", "seq", None, "guide"),
            P("group"),
            P("group", None),
        ),
        out_specs=P("group", "seq", None, "guide"),
        check_vma=False,
    )
```

```python
import functools
import math

import jax
import jax.numpy as jnp
from jax import lax
from jax.experimental import pallas as pl
from jax.experimental.pallas import tpu as pltpu
from jax.sharding import PartitionSpec as P

HEAD_DIM = 128
MESH = pl.DeviceIdType.MESH

beta_low = 0.0001
beta_high = 0.02
guidance_scale = 3.0
norm_epsilon = 1e-06


def plan_weight(timesteps):
    steps_float = timesteps.astype(jnp.float32)
    exponent = (steps_float + 1.0) * beta_low + (beta_high - beta_low) * steps_float * (
        steps_float + 1.0
    ) / (2.0 * 999.0)
    return 1.0 - jnp.exp(-exponent)


def attend(q, k, v):
    scores = lax.dot_general(q, k, (((1,), (1,)), ((), ())), preferred_element_type=jnp.float32)
    top = jnp.max(scores, axis=-1, keepdims=True)
    expo = jnp.exp2((scores - top) * (HEAD_DIM ** (-0.5) * math.log2(math.e)))
    denom = jnp.sum(expo, axis=-1, keepdims=True)
    mixed = jnp.dot(expo.astype(jnp.bfloat16), v, preferred_element_type=jnp.float32)
    return (mixed / denom).astype(jnp.bfloat16)


def kernel(
    n_seq, n_shard, width_all, chunk,
    q_hbm, k_hbm, v_hbm, res_hbm, w_hbm, gate_hbm, shift_hbm, scale_hbm, wh_hbm, noise_hbm,
    steps_hbm, owner_hbm, out_ref,
    qkv, left, q_left, att, ostage, w_vm, res_vm, vec_vm, wh_vm, noise_vm, steps_vm, owner_vm,
    psend, pbuf, msg, gbuf, fsend,
    z_send, z_recv, l_send, l_recv, o_send, o_recv, a_send, a_recv,
    p_send, p_recv, m_send, m_recv, f_send, f_recv, in_sem, own_sem,
):
    z, s, g = lax.axis_index("seq"), lax.axis_index("shard"), lax.axis_index("guide")
    rows, width = q_hbm.shape
    heads = width // HEAD_DIM
    n_full = heads // n_seq
    n_left = heads - n_full * n_seq
    left_at = n_full * n_seq * HEAD_DIM
    half = w_hbm.shape[1]
    feats = res_hbm.shape[1]
    per = half // feats
    n_chunk = feats // chunk
    channels = wh_hbm.shape[0]
    n_frame = owner_hbm.shape[1]
    frame_rows = rows // n_frame

    def head_cols(index):
        return pl.ds(pl.multiple_of(index * HEAD_DIM, HEAD_DIM), HEAD_DIM)

    def block_rows(index):
        return pl.ds(pl.multiple_of(index * rows, rows), rows)

    def ahead(d):
        return lax.rem(z + d, n_seq)

    def behind(d):
        return lax.rem(z + n_seq - d, n_seq)

    own = []
    tensors = (q_hbm, k_hbm, v_hbm)
    for a in range(n_full):
        for t in range(3):
            own.append(pltpu.make_async_copy(
                tensors[t].at[:, head_cols(z * n_full + a)], qkv.at[a, t, block_rows(z)],
                own_sem.at[a * 3 + t]))
    if n_left:
        for t in range(2):
            own.append(pltpu.make_async_copy(
                tensors[t + 1].at[:, pl.ds(left_at, n_left * HEAD_DIM)], left.at[t, block_rows(z)],
                own_sem.at[n_full * 3 + t]))
        own.append(pltpu.make_async_copy(
            q_hbm.at[:, pl.ds(left_at, n_left * HEAD_DIM)], q_left, own_sem.at[n_full * 3 + 2]))
    loads = [
        pltpu.make_async_copy(gate_hbm, vec_vm.at[0], in_sem.at[0]),
        pltpu.make_async_copy(shift_hbm, vec_vm.at[1], in_sem.at[1]),
        pltpu.make_async_copy(scale_hbm, vec_vm.at[2], in_sem.at[2]),
        pltpu.make_async_copy(wh_hbm, wh_vm, in_sem.at[3]),
        pltpu.make_async_copy(noise_hbm, noise_vm, in_sem.at[4]),
        pltpu.make_async_copy(res_hbm, res_vm, in_sem.at[5]),
        pltpu.make_async_copy(steps_hbm, steps_vm, in_sem.at[6]),
        pltpu.make_async_copy(owner_hbm, owner_vm, in_sem.at[7]),
        pltpu.make_async_copy(w_hbm, w_vm, in_sem.at[8]),
    ]

    barrier = pltpu.get_barrier_semaphore()
    for d in range(1, n_seq):
        pl.semaphore_signal(barrier, inc=1, device_id={"seq": ahead(d)}, device_id_type=MESH)
    n_local = 2 * n_shard
    me_local = s * 2 + g

    def local_peer(d):
        index = lax.rem(me_local + d, n_local)
        return {"shard": index // 2, "guide": index % 2}

    for d in range(1, n_local):
        pl.semaphore_signal(barrier, inc=1, device_id=local_peer(d), device_id_type=MESH)
    for copy in own:
        copy.start()
    pl.semaphore_wait(barrier, n_seq - 1 + n_local - 1)

    order = sorted(range(1, n_seq), key=lambda d: -min(d, n_seq - d))
    z_copies = {}
    for a in range(n_full):
        for d in order:
            for t in range(3):
                copy = pltpu.make_async_remote_copy(
                    src_ref=tensors[t].at[:, head_cols(ahead(d) * n_full + a)],
                    dst_ref=qkv.at[a, t, block_rows(z)],
                    send_sem=z_send.at[a, t, d - 1], recv_sem=z_recv.at[a, t, d - 1],
                    device_id={"seq": ahead(d)}, device_id_type=MESH)
                copy.start()
                z_copies[a, d, t] = copy
    l_copies = []
    if n_left:
        for d in order:
            for t in range(2):
                copy = pltpu.make_async_remote_copy(
                    src_ref=tensors[t + 1].at[:, pl.ds(left_at, n_left * HEAD_DIM)],
                    dst_ref=left.at[t, block_rows(z)],
                    send_sem=l_send.at[t, d - 1], recv_sem=l_recv.at[t, d - 1],
                    device_id={"seq": ahead(d)}, device_id_type=MESH)
                copy.start()
                l_copies.append(copy)
    for copy in loads:
        copy.start()

    for copy in loads[:8]:
        copy.wait()
    gains = jnp.concatenate([1.0 + vec_vm[2], vec_vm[1]], axis=0)
    consts = lax.dot_general(
        gains, wh_vm[...].astype(jnp.float32), (((1,), (1,)), ((), ())),
        precision=lax.Precision.HIGHEST, preferred_element_type=jnp.float32)
    msg[me_local, rows:, :] = jnp.zeros((8, msg.shape[2]), jnp.float32)
    msg[me_local, rows : rows + 2, 0:channels] = consts
    for copy in own:
        copy.wait()

    o_copies = []
    for a in range(n_full):
        for d in range(1, n_seq):
            for t in range(3):
                z_copies[a, d, t].wait_recv()
        for d in order + [0]:
            to = ahead(d)
            mixed = attend(qkv[a, 0, block_rows(to)], qkv[a, 1], qkv[a, 2])
            cols = head_cols(z * n_full + a)
            if d == 0:
                att[g, :, cols] = mixed
            else:
                ostage[a, d - 1] = mixed
                copy = pltpu.make_async_remote_copy(
                    src_ref=ostage.at[a, d - 1], dst_ref=att.at[g, :, cols],
                    send_sem=o_send.at[a, d - 1], recv_sem=o_recv.at[a, d - 1],
                    device_id={"seq": to}, device_id_type=MESH)
                copy.start()
                o_copies.append(copy)
    for copy in l_copies:
        copy.wait_recv()
    for h in range(n_left):
        cols = pl.ds(h * HEAD_DIM, HEAD_DIM)
        att[g, :, pl.ds(left_at + h * HEAD_DIM, HEAD_DIM)] = attend(
            q_left[:, cols], left[0, :, cols], left[1, :, cols])
    for a in range(n_full):
        for d in range(1, n_seq):
            pltpu.make_async_remote_copy(
                src_ref=ostage.at[a, d - 1], dst_ref=att.at[g, :, head_cols(behind(d) * n_full + a)],
                send_sem=o_send.at[a, d - 1], recv_sem=o_recv.at[a, d - 1],
                device_id={"seq": ahead(d)}, device_id_type=MESH).wait_recv()

    swap = pltpu.make_async_remote_copy(
        src_ref=att.at[g], dst_ref=att.at[g], send_sem=a_send, recv_sem=a_recv,
        device_id={"guide": 1 - g}, device_id_type=MESH)
    swap.start()
    loads[8].wait()
    swap.wait_recv()

    def p_copy(b, q, c):
        return pltpu.make_async_remote_copy(
            src_ref=psend.at[b, q, c], dst_ref=pbuf.at[s, c],
            send_sem=p_send.at[b, q, c], recv_sem=p_recv.at[s, c],
            device_id={"shard": g * per + q, "guide": b}, device_id_type=MESH)

    def is_me(b, q):
        return jnp.logical_and(g == b, g * per + q == s)

    both = jnp.concatenate([att[0], att[1]], axis=0)
    for c in range(n_chunk):
        for q in range(per):
            part = jnp.dot(
                both, w_vm[:, q * feats + c * chunk : q * feats + (c + 1) * chunk],
                preferred_element_type=jnp.float32).astype(jnp.bfloat16)
            for b in range(2):
                psend[b, q, c] = part[b * rows : (b + 1) * rows]

                @pl.when(is_me(b, q))
                def _():
                    pbuf[s, c] = psend[b, q, c]

                @pl.when(jnp.logical_not(is_me(b, q)))
                def _():
                    p_copy(b, q, c).start()

    from_guide = s // per
    first = jnp.zeros((rows, 1), jnp.float32)
    second = jnp.zeros((rows, 1), jnp.float32)
    head = jnp.zeros((rows, channels), jnp.float32)
    for c in range(n_chunk):
        for r in range(n_shard):

            @pl.when(jnp.logical_not(jnp.logical_and(from_guide == g, s == r)))
            def _():
                pltpu.make_async_remote_copy(
                    src_ref=psend.at[0, 0, c], dst_ref=pbuf.at[r, c],
                    send_sem=p_send.at[0, 0, c], recv_sem=p_recv.at[r, c],
                    device_id={"guide": 1 - g}, device_id_type=MESH).wait_recv()

        at = slice(c * chunk, (c + 1) * chunk)
        total = pbuf[0, c].astype(jnp.float32)
        for r in range(1, n_shard):
            total = total + pbuf[r, c].astype(jnp.float32)
        hidden = res_vm[:, at].astype(jnp.float32) + vec_vm[0, :, at] * total
        first = first + jnp.sum(hidden, axis=-1, keepdims=True)
        second = second + jnp.sum(hidden * hidden, axis=-1, keepdims=True)
        gained = hidden * (1.0 + vec_vm[2, :, at])
        high = gained.astype(jnp.bfloat16)
        rest = gained - high.astype(jnp.float32)
        low = rest.astype(jnp.bfloat16)
        last = (rest - low.astype(jnp.float32)).astype(jnp.bfloat16)
        wh = wh_vm[:, at]
        for piece in (last, low, high):
            head = head + lax.dot_general(
                piece, wh, (((1,), (1,)), ((), ())), preferred_element_type=jnp.float32)
    msg[me_local, 0:rows, 0:channels] = head
    tail = msg.shape[2] - channels
    lane = lax.broadcasted_iota(jnp.int32, (rows, tail), 1)
    msg[me_local, 0:rows, channels:] = jnp.where(lane == 0, first, second)
    m_copies = []
    for d in range(1, n_local):
        copy = pltpu.make_async_remote_copy(
            src_ref=msg.at[me_local], dst_ref=msg.at[me_local],
            send_sem=m_send.at[d - 1], recv_sem=m_recv.at[d - 1],
            device_id=local_peer(d), device_id_type=MESH)
        copy.start()
        m_copies.append(copy)
    for copy in m_copies:
        copy.wait_recv()

    eps = []
    for b in range(2):
        total = msg[b]
        for r in range(1, n_shard):
            total = total + msg[r * 2 + b]
        mean = total[0:rows, channels : channels + 1] / width_all
        var = total[0:rows, channels + 1 : channels + 2] / width_all - mean * mean
        inv = lax.rsqrt(var + norm_epsilon)
        eps.append(
            (total[0:rows, 0:channels] - mean * total[rows : rows + 1, 0:channels]) * inv
            + total[rows + 1 : rows + 2, 0:channels])
    guided = eps[1] + guidance_scale * (eps[0] - eps[1])

    f_copies = []
    for d in order + [0]:
        to = ahead(d)
        picked = jnp.zeros((frame_rows, channels), jnp.float32)
        for f in range(n_frame):
            hit = owner_vm[:, f : f + 1] == to
            picked = picked + jnp.where(hit, guided[f * frame_rows : (f + 1) * frame_rows], 0.0)
        if d == 0:
            gbuf[z] = picked
        else:
            fsend[d - 1] = picked
            copy = pltpu.make_async_remote_copy(
                src_ref=fsend.at[d - 1], dst_ref=gbuf.at[z],
                send_sem=f_send.at[d - 1], recv_sem=f_recv.at[d - 1],
                device_id={"seq": to}, device_id_type=MESH)
            copy.start()
            f_copies.append(copy)
    out_ch = channels // 2
    weight = plan_weight(jnp.full((1, rows), steps_vm[0], jnp.int32))
    for copy in f_copies:
        copy.wait_recv()
    frame = gbuf[...].reshape(n_seq * frame_rows, channels).T
    is_first = jnp.full((out_ch, 1), g, jnp.int32) == 0
    mine = jnp.where(is_first, frame[0:out_ch], frame[out_ch:])
    out_ref[...] = weight * (mine - noise_vm[...])

    for copy in list(z_copies.values()) + l_copies + o_copies + m_copies + f_copies + [swap]:
        copy.wait_send()
    for c in range(n_chunk):
        for q in range(per):
            for b in range(2):

                @pl.when(jnp.logical_not(is_me(b, q)))
                def _():
                    p_copy(b, q, c).wait_send()


def on_device(
    n_seq, n_shard,
    queries, key_vecs, value_vecs, residual, w_out, attn_gate, norm_shift, norm_scale, w_head,
    noise, timesteps, frame_owner,
):
    rows, width = queries.shape[2:]
    heads = width // HEAD_DIM
    n_full = heads // n_seq
    n_left = heads - n_full * n_seq
    half = w_out.shape[1]
    feats = residual.shape[3]
    per = half // feats
    chunk = next(size for size in (512, 256, 128) if feats % size == 0)
    n_chunk = feats // chunk
    channels = w_head.shape[1]
    n_frame = frame_owner.shape[1]
    frame_rows = rows // n_frame
    noise_t = noise[0, 0].T
    n_local = 2 * n_shard
    bf16, f32 = jnp.bfloat16, jnp.float32
    full1, left1 = max(n_full, 1), max(n_left, 1)
    dma = pltpu.SemaphoreType.DMA
    hbm = pl.BlockSpec(memory_space=pltpu.HBM)
    out = pl.pallas_call(
        functools.partial(kernel, n_seq, n_shard, feats * n_shard, chunk),
        out_shape=jax.ShapeDtypeStruct(noise_t.shape, f32),
        in_specs=[hbm] * 12,
        out_specs=pl.BlockSpec(memory_space=pltpu.VMEM),
        scratch_shapes=[
            pltpu.VMEM((full1, 3, n_seq * rows, HEAD_DIM), bf16),
            pltpu.VMEM((2, n_seq * rows, left1 * HEAD_DIM), bf16),
            pltpu.VMEM((rows, left1 * HEAD_DIM), bf16),
            pltpu.VMEM((2, rows, width), bf16),
            pltpu.VMEM((full1, n_seq - 1, rows, HEAD_DIM), bf16),
            pltpu.VMEM(w_out.shape, bf16),
            pltpu.VMEM((rows, feats), bf16),
            pltpu.VMEM((3, 1, feats), f32),
            pltpu.VMEM((channels, feats), bf16),
            pltpu.VMEM(noise_t.shape, f32),
            pltpu.SMEM((1,), jnp.int32),
            pltpu.VMEM((1, n_frame), jnp.int32),
            pltpu.VMEM((2, per, n_chunk, rows, chunk), bf16),
            pltpu.VMEM((n_shard, n_chunk, rows, chunk), bf16),
            pltpu.VMEM((n_local, rows + 8, 128), f32),
            pltpu.VMEM((n_seq, frame_rows, channels), f32),
            pltpu.VMEM((n_seq - 1, frame_rows, channels), f32),
            dma((full1, 3, n_seq - 1)), dma((full1, 3, n_seq - 1)),
            dma((2, n_seq - 1)), dma((2, n_seq - 1)),
            dma((full1, n_seq - 1)), dma((full1, n_seq - 1)),
            dma, dma,
            dma((2, per, n_chunk)), dma((n_shard, n_chunk)),
            dma((n_local - 1,)), dma((n_local - 1,)),
            dma((n_seq - 1,)), dma((n_seq - 1,)),
            dma((9,)), dma((n_full * 3 + 3,)),
        ],
        compiler_params=pltpu.CompilerParams(
            collective_id=0, has_side_effects=True, vmem_limit_bytes=63 * 1024 * 1024),
    )(
        queries[0, 0], key_vecs[0, 0], value_vecs[0, 0], residual[0, 0], w_out,
        attn_gate, norm_shift, norm_scale, w_head.T, noise_t, timesteps, frame_owner,
    )
    return out.T[None, None]


def solution(mesh):
    return jax.shard_map(
        functools.partial(on_device, mesh.shape["seq"], mesh.shape["shard"]),
        mesh=mesh,
        in_specs=(
            P("guide", "group", "seq", "shard"),
            P("guide", "group", "seq", "shard"),
            P("guide", "group", "seq", "shard"),
            P("guide", "group", "seq", "shard"),
            P("shard", "guide"),
            P("group", "shard"),
            P("group", "shard"),
            P("group", "shard"),
            P("shard", None),
            P("group", "seq", None, "guide"),
            P("group"),
            P("group", None),
        ),
        out_specs=P("group", "seq", None, "guide"),
        check_vma=False,
    )
```

```python
import functools
import math

import jax
import jax.numpy as jnp
from jax import lax
from jax.experimental import pallas as pl
from jax.experimental.pallas import tpu as pltpu
from jax.sharding import PartitionSpec as P

HEAD_DIM = 128
MESH = pl.DeviceIdType.MESH

beta_low = 0.0001
beta_high = 0.02
guidance_scale = 3.0
norm_epsilon = 1e-06


def plan_weight(timesteps):
    steps_float = timesteps.astype(jnp.float32)
    exponent = (steps_float + 1.0) * beta_low + (beta_high - beta_low) * steps_float * (
        steps_float + 1.0
    ) / (2.0 * 999.0)
    return 1.0 - jnp.exp(-exponent)


def attend(q, k, v):
    scores = lax.dot_general(q, k, (((1,), (1,)), ((), ())), preferred_element_type=jnp.float32)
    top = jnp.max(scores, axis=-1, keepdims=True)
    expo = jnp.exp2((scores - top) * (HEAD_DIM ** (-0.5) * math.log2(math.e)))
    denom = jnp.sum(expo, axis=-1, keepdims=True)
    mixed = jnp.dot(expo.astype(jnp.bfloat16), v, preferred_element_type=jnp.float32)
    return (mixed / denom).astype(jnp.bfloat16)


def kernel(
    n_seq, n_shard, width_all, chunk,
    q_hbm, k_hbm, v_hbm, res_hbm, w_hbm, gate_hbm, shift_hbm, scale_hbm, wh_hbm, noise_hbm,
    steps_hbm, owner_hbm, out_ref,
    qkv, left, q_left, att, ostage, w_vm, res_vm, vec_vm, wh_vm, noise_vm, steps_vm, owner_vm,
    psend, pbuf, msg, gbuf, fsend,
    z_send, z_recv, l_send, l_recv, o_send, o_recv, a_send, a_recv,
    p_send, p_recv, m_send, m_recv, f_send, f_recv, in_sem, own_sem,
):
    z, s, g = lax.axis_index("seq"), lax.axis_index("shard"), lax.axis_index("guide")
    rows, width = q_hbm.shape
    heads = width // HEAD_DIM
    n_full = heads // n_seq
    n_left = heads - n_full * n_seq
    left_at = n_full * n_seq * HEAD_DIM
    half = w_hbm.shape[1]
    feats = res_hbm.shape[1]
    per = half // feats
    n_chunk = feats // chunk
    channels = wh_hbm.shape[0]
    n_frame = owner_hbm.shape[1]
    frame_rows = rows // n_frame

    def head_cols(index):
        return pl.ds(pl.multiple_of(index * HEAD_DIM, HEAD_DIM), HEAD_DIM)

    def block_rows(index):
        return pl.ds(pl.multiple_of(index * rows, rows), rows)

    def ahead(d):
        return lax.rem(z + d, n_seq)

    def behind(d):
        return lax.rem(z + n_seq - d, n_seq)

    own = []
    tensors = (q_hbm, k_hbm, v_hbm)
    for a in range(n_full):
        for t in range(3):
            own.append(pltpu.make_async_copy(
                tensors[t].at[:, head_cols(z * n_full + a)], qkv.at[a, t, block_rows(z)],
                own_sem.at[a * 3 + t]))
    if n_left:
        for t in range(2):
            own.append(pltpu.make_async_copy(
                tensors[t + 1].at[:, pl.ds(left_at, n_left * HEAD_DIM)], left.at[t, block_rows(z)],
                own_sem.at[n_full * 3 + t]))
        own.append(pltpu.make_async_copy(
            q_hbm.at[:, pl.ds(left_at, n_left * HEAD_DIM)], q_left, own_sem.at[n_full * 3 + 2]))
    loads = [
        pltpu.make_async_copy(gate_hbm, vec_vm.at[0], in_sem.at[0]),
        pltpu.make_async_copy(shift_hbm, vec_vm.at[1], in_sem.at[1]),
        pltpu.make_async_copy(scale_hbm, vec_vm.at[2], in_sem.at[2]),
        pltpu.make_async_copy(wh_hbm, wh_vm, in_sem.at[3]),
        pltpu.make_async_copy(noise_hbm, noise_vm, in_sem.at[4]),
        pltpu.make_async_copy(res_hbm, res_vm, in_sem.at[5]),
        pltpu.make_async_copy(steps_hbm, steps_vm, in_sem.at[6]),
        pltpu.make_async_copy(owner_hbm, owner_vm, in_sem.at[7]),
        pltpu.make_async_copy(w_hbm, w_vm, in_sem.at[8]),
    ]

    barrier = pltpu.get_barrier_semaphore()
    for d in range(1, n_seq):
        pl.semaphore_signal(barrier, inc=1, device_id={"seq": ahead(d)}, device_id_type=MESH)
    n_local = 2 * n_shard
    me_local = s * 2 + g

    def local_peer(d):
        index = lax.rem(me_local + d, n_local)
        return {"shard": index // 2, "guide": index % 2}

    for d in range(1, n_local):
        pl.semaphore_signal(barrier, inc=1, device_id=local_peer(d), device_id_type=MESH)
    for copy in own:
        copy.start()
    pl.semaphore_wait(barrier, n_seq - 1 + n_local - 1)

    def relay(t, side, step):
        rows_from = block_rows(z - step if side == 0 else z + step)
        source = left.at[t, rows_from]
        if step == 0:
            source = tensors[t + 1].at[:, pl.ds(left_at, n_left * HEAD_DIM)]
        return pltpu.make_async_remote_copy(
            src_ref=source, dst_ref=left.at[t, rows_from],
            send_sem=l_send.at[t, side, step], recv_sem=l_recv.at[t, side, step],
            device_id={"seq": z + 1 if side == 0 else z - 1}, device_id_type=MESH)

    def relay_each(act, step):
        for side in range(2):
            at_source = z if side == 0 else n_seq - 1 - z
            sends = jnp.logical_and(at_source >= step, at_source < n_seq - 1)
            receives = at_source >= step + 1

            @pl.when(receives if act == "wait_recv" else sends)
            def _():
                for t in range(2):
                    getattr(relay(t, side, step), act)()

    order = sorted(range(1, n_seq), key=lambda d: -min(d, n_seq - d))
    z_copies = {}

    def send_head(a):
        for d in order:
            for t in range(3):
                copy = pltpu.make_async_remote_copy(
                    src_ref=tensors[t].at[:, head_cols(ahead(d) * n_full + a)],
                    dst_ref=qkv.at[a, t, block_rows(z)],
                    send_sem=z_send.at[a, t, d - 1], recv_sem=z_recv.at[a, t, d - 1],
                    device_id={"seq": ahead(d)}, device_id_type=MESH)
                copy.start()
                z_copies[a, d, t] = copy

    if n_left:
        relay_each("start", 0)
    if n_full:
        send_head(0)
    for copy in loads:
        copy.start()

    for copy in loads[:8]:
        copy.wait()
    gains = jnp.concatenate([1.0 + vec_vm[2], vec_vm[1]], axis=0)
    consts = lax.dot_general(
        gains, wh_vm[...].astype(jnp.float32), (((1,), (1,)), ((), ())),
        precision=lax.Precision.HIGHEST, preferred_element_type=jnp.float32)
    msg[me_local, channels + 8 :, :] = jnp.zeros((8, rows), jnp.float32)
    msg[me_local, channels + 8 : channels + 10, 0:channels] = consts
    for copy in own:
        copy.wait()

    if n_left:
        for step in range(n_seq - 2):
            relay_each("wait_recv", step)
            relay_each("start", step + 1)
    for a in range(1, n_full):
        for d in order:
            for t in range(3):
                z_copies[a - 1, d, t].wait_send()
        send_head(a)

    def attend_left():
        relay_each("wait_recv", n_seq - 2)
        for h in range(n_left):
            cols = pl.ds(h * HEAD_DIM, HEAD_DIM)
            att[g, :, pl.ds(left_at + h * HEAD_DIM, HEAD_DIM)] = attend(
                q_left[:, cols], left[0, :, cols], left[1, :, cols])

    o_copies = []
    for a in range(n_full):
        for d in range(1, n_seq):
            for t in range(3):
                z_copies[a, d, t].wait_recv()
        for d in order + [0]:
            to = ahead(d)
            mixed = attend(qkv[a, 0, block_rows(to)], qkv[a, 1], qkv[a, 2])
            cols = head_cols(z * n_full + a)
            if d == 0:
                att[g, :, cols] = mixed
            else:
                ostage[a, d - 1] = mixed
                copy = pltpu.make_async_remote_copy(
                    src_ref=ostage.at[a, d - 1], dst_ref=att.at[g, :, cols],
                    send_sem=o_send.at[a, d - 1], recv_sem=o_recv.at[a, d - 1],
                    device_id={"seq": to}, device_id_type=MESH)
                copy.start()
                o_copies.append(copy)
        if a == 0 and n_left:
            attend_left()
    if not n_full:
        attend_left()
    for a in range(n_full):
        for d in range(1, n_seq):
            pltpu.make_async_remote_copy(
                src_ref=ostage.at[a, d - 1], dst_ref=att.at[g, :, head_cols(behind(d) * n_full + a)],
                send_sem=o_send.at[a, d - 1], recv_sem=o_recv.at[a, d - 1],
                device_id={"seq": ahead(d)}, device_id_type=MESH).wait_recv()

    swap = pltpu.make_async_remote_copy(
        src_ref=att.at[g], dst_ref=att.at[g], send_sem=a_send, recv_sem=a_recv,
        device_id={"guide": 1 - g}, device_id_type=MESH)
    swap.start()
    loads[8].wait()

    def p_copy(b, q, c):
        return pltpu.make_async_remote_copy(
            src_ref=psend.at[b, q, c], dst_ref=pbuf.at[s, c],
            send_sem=p_send.at[b, q, c], recv_sem=p_recv.at[s, c],
            device_id={"shard": g * per + q, "guide": b}, device_id_type=MESH)

    def is_me(b, q):
        return jnp.logical_and(g == b, g * per + q == s)

    for b in (g, 1 - g):
        if b is not g:
            swap.wait_recv()
        for c in range(n_chunk):
            for q in range(per):
                psend[b, q, c] = jnp.dot(
                    att[b], w_vm[:, q * feats + c * chunk : q * feats + (c + 1) * chunk],
                    preferred_element_type=jnp.float32).astype(jnp.bfloat16)

                @pl.when(is_me(b, q))
                def _():
                    pbuf[s, c] = psend[b, q, c]

                @pl.when(jnp.logical_not(is_me(b, q)))
                def _():
                    p_copy(b, q, c).start()

    from_guide = s // per
    first = jnp.zeros((rows, 1), jnp.float32)
    second = jnp.zeros((rows, 1), jnp.float32)
    head = jnp.zeros((channels, rows), jnp.float32)
    for c in range(n_chunk):
        for r in range(n_shard):

            @pl.when(jnp.logical_not(jnp.logical_and(from_guide == g, s == r)))
            def _():
                pltpu.make_async_remote_copy(
                    src_ref=psend.at[0, 0, c], dst_ref=pbuf.at[r, c],
                    send_sem=p_send.at[0, 0, c], recv_sem=p_recv.at[r, c],
                    device_id={"guide": 1 - g}, device_id_type=MESH).wait_recv()

        at = slice(c * chunk, (c + 1) * chunk)
        total = pbuf[0, c].astype(jnp.float32)
        for r in range(1, n_shard):
            total = total + pbuf[r, c].astype(jnp.float32)
        hidden = res_vm[:, at].astype(jnp.float32) + vec_vm[0, :, at] * total
        first = first + jnp.sum(hidden, axis=-1, keepdims=True)
        second = second + jnp.sum(hidden * hidden, axis=-1, keepdims=True)
        gained = hidden * (1.0 + vec_vm[2, :, at])
        high = gained.astype(jnp.bfloat16)
        rest = gained - high.astype(jnp.float32)
        low = rest.astype(jnp.bfloat16)
        last = (rest - low.astype(jnp.float32)).astype(jnp.bfloat16)
        wh = wh_vm[:, at]
        for piece in (last, low, high):
            head = head + lax.dot_general(
                wh, piece, (((1,), (1,)), ((), ())), preferred_element_type=jnp.float32)
    msg[me_local, 0:channels, :] = head
    lane = lax.broadcasted_iota(jnp.int32, (rows, rows), 1)
    msg[me_local, channels : channels + 8, :] = jnp.where(lane == 0, first, second).T[0:8]
    m_copies = []
    for d in range(1, n_local):
        copy = pltpu.make_async_remote_copy(
            src_ref=msg.at[me_local], dst_ref=msg.at[me_local],
            send_sem=m_send.at[d - 1], recv_sem=m_recv.at[d - 1],
            device_id=local_peer(d), device_id_type=MESH)
        copy.start()
        m_copies.append(copy)
    for copy in m_copies:
        copy.wait_recv()

    eps = []
    for b in range(2):
        total = msg[b]
        for r in range(1, n_shard):
            total = total + msg[r * 2 + b]
        mean = total[channels : channels + 1] / width_all
        var = total[channels + 1 : channels + 2] / width_all - mean * mean
        inv = lax.rsqrt(var + norm_epsilon)
        fixed = total[channels + 8 :].T[0:channels]
        eps.append((total[0:channels] - fixed[:, 0:1] * mean) * inv + fixed[:, 1:2])
    guided = (eps[1] + guidance_scale * (eps[0] - eps[1])).T

    f_copies = []
    for d in order + [0]:
        to = ahead(d)
        picked = jnp.zeros((frame_rows, channels), jnp.float32)
        for f in range(n_frame):
            hit = owner_vm[:, f : f + 1] == to
            picked = picked + jnp.where(hit, guided[f * frame_rows : (f + 1) * frame_rows], 0.0)
        if d == 0:
            gbuf[z] = picked
        else:
            fsend[d - 1] = picked
            copy = pltpu.make_async_remote_copy(
                src_ref=fsend.at[d - 1], dst_ref=gbuf.at[z],
                send_sem=f_send.at[d - 1], recv_sem=f_recv.at[d - 1],
                device_id={"seq": to}, device_id_type=MESH)
            copy.start()
            f_copies.append(copy)
    out_ch = channels // 2
    weight = plan_weight(jnp.full((1, rows), steps_vm[0], jnp.int32))
    for copy in f_copies:
        copy.wait_recv()
    frame = gbuf[...].reshape(n_seq * frame_rows, channels).T
    is_first = jnp.full((out_ch, 1), g, jnp.int32) == 0
    mine = jnp.where(is_first, frame[0:out_ch], frame[out_ch:])
    out_ref[...] = weight * (mine - noise_vm[...])

    last = [copy for (a, _, _), copy in z_copies.items() if a == n_full - 1]
    if n_left:
        for step in range(n_seq - 1):
            relay_each("wait_send", step)
    for copy in last + o_copies + m_copies + f_copies + [swap]:
        copy.wait_send()
    for c in range(n_chunk):
        for q in range(per):
            for b in range(2):

                @pl.when(jnp.logical_not(is_me(b, q)))
                def _():
                    p_copy(b, q, c).wait_send()


def on_device(
    n_seq, n_shard,
    queries, key_vecs, value_vecs, residual, w_out, attn_gate, norm_shift, norm_scale, w_head,
    noise, timesteps, frame_owner,
):
    rows, width = queries.shape[2:]
    heads = width // HEAD_DIM
    n_full = heads // n_seq
    n_left = heads - n_full * n_seq
    half = w_out.shape[1]
    feats = residual.shape[3]
    per = half // feats
    chunk = next(size for size in (512, 256, 128) if feats % size == 0)
    n_chunk = feats // chunk
    channels = w_head.shape[1]
    n_frame = frame_owner.shape[1]
    frame_rows = rows // n_frame
    noise_t = noise[0, 0].T
    n_local = 2 * n_shard
    bf16, f32 = jnp.bfloat16, jnp.float32
    full1, left1 = max(n_full, 1), max(n_left, 1)
    dma = pltpu.SemaphoreType.DMA
    hbm = pl.BlockSpec(memory_space=pltpu.HBM)
    out = pl.pallas_call(
        functools.partial(kernel, n_seq, n_shard, feats * n_shard, chunk),
        out_shape=jax.ShapeDtypeStruct(noise_t.shape, f32),
        in_specs=[hbm] * 12,
        out_specs=pl.BlockSpec(memory_space=pltpu.VMEM),
        scratch_shapes=[
            pltpu.VMEM((full1, 3, n_seq * rows, HEAD_DIM), bf16),
            pltpu.VMEM((2, n_seq * rows, left1 * HEAD_DIM), bf16),
            pltpu.VMEM((rows, left1 * HEAD_DIM), bf16),
            pltpu.VMEM((2, rows, width), bf16),
            pltpu.VMEM((full1, n_seq - 1, rows, HEAD_DIM), bf16),
            pltpu.VMEM(w_out.shape, bf16),
            pltpu.VMEM((rows, feats), bf16),
            pltpu.VMEM((3, 1, feats), f32),
            pltpu.VMEM((channels, feats), bf16),
            pltpu.VMEM(noise_t.shape, f32),
            pltpu.SMEM((1,), jnp.int32),
            pltpu.VMEM((1, n_frame), jnp.int32),
            pltpu.VMEM((2, per, n_chunk, rows, chunk), bf16),
            pltpu.VMEM((n_shard, n_chunk, rows, chunk), bf16),
            pltpu.VMEM((n_local, channels + 16, rows), f32),
            pltpu.VMEM((n_seq, frame_rows, channels), f32),
            pltpu.VMEM((n_seq - 1, frame_rows, channels), f32),
            dma((full1, 3, n_seq - 1)), dma((full1, 3, n_seq - 1)),
            dma((2, 2, n_seq - 1)), dma((2, 2, n_seq - 1)),
            dma((full1, n_seq - 1)), dma((full1, n_seq - 1)),
            dma, dma,
            dma((2, per, n_chunk)), dma((n_shard, n_chunk)),
            dma((n_local - 1,)), dma((n_local - 1,)),
            dma((n_seq - 1,)), dma((n_seq - 1,)),
            dma((9,)), dma((n_full * 3 + 3,)),
        ],
        compiler_params=pltpu.CompilerParams(
            collective_id=0, has_side_effects=True, vmem_limit_bytes=63 * 1024 * 1024),
    )(
        queries[0, 0], key_vecs[0, 0], value_vecs[0, 0], residual[0, 0], w_out,
        attn_gate, norm_shift, norm_scale, w_head.T, noise_t, timesteps, frame_owner,
    )
    return out.T[None, None]


def solution(mesh):
    return jax.shard_map(
        functools.partial(on_device, mesh.shape["seq"], mesh.shape["shard"]),
        mesh=mesh,
        in_specs=(
            P("guide", "group", "seq", "shard"),
            P("guide", "group", "seq", "shard"),
            P("guide", "group", "seq", "shard"),
            P("guide", "group", "seq", "shard"),
            P("shard", "guide"),
            P("group", "shard"),
            P("group", "shard"),
            P("group", "shard"),
            P("shard", None),
            P("group", "seq", None, "guide"),
            P("group"),
            P("group", None),
        ),
        out_specs=P("group", "seq", None, "guide"),
        check_vma=False,
    )
```
